256 devices in a mesh: tensor: 4 (over x_lo, core), token: 32 (over z, y), dp: 2 (over x_hi).
Axes of the slice: x: 4 (x_hi: 2, x_lo: 2; x = x_hi * 2 + x_lo), y: 4, z: 8, core: 2. Of those that a mesh axis runs over, the one named last changes fastest.
Arguments:
- hidden_in: bfloat16 [32768, 8192], P(('token', 'dp'), 'tensor'), may hold values from -6 to 6
- sender_cache: bfloat16 [32768, 2048], P(('token', 'dp'), 'tensor'), may hold values from -6 to 6
- block_slot: int32 [32], P('token'), may hold values from 0 to 31, each once
- norm_gain: float32 [8192], P('tensor'), may hold values from 0.1 to 1.9
- kv_weight: bfloat16 [8192, 2, 1024], P('token', None, 'tensor'), may hold values from -0.0625 to 0.0625
- proj_in: bfloat16 [2048, 2048], P(('token', 'dp'), 'tensor'), may hold values from -0.125 to 0.125
- proj_out: bfloat16 [2048, 2, 1024], P(('tensor', 'token', 'dp')), may hold values from -0.125 to 0.125
Outputs:
- grad_in: float32 [2048, 2048], P(('token', 'dp'), 'tensor')
- grad_out: float32 [2048, 2, 1024], P(('tensor', 'token', 'dp'))
The draws below stay inside these ranges and needn't reach their ends.
Inputs may be any that keep to these rules, and one draw needn't show every extreme that they name: `block_slot`: each slot of a sequence appears once.
All inputs are finite; a program needn't handle non-finite values.
Results may differ from the reference program's by a relative error of at most 0.015.
Values may be sent and summed in bfloat16 or wider, within the bound.
No kernel may reach another device: no remote copies, remote signals or barrier semaphores. Data moves between devices by JAX's collectives and lax.ppermute only.
A program may use at most 128 MiB of HBM per device.

```python
import jax
import jax.numpy as jnp
from jax import lax

D = 8192
KV = 1024
HD = 128
SK = 2048
F = 2048
TOK_DEV = 512
SPANS = 32
TOKENS = 32768
N_DP = 2


def levels(own_key, dims, cuts, smallest, largest):
    factor_of, own = 1.0, jax.random.fold_in(own_key, 6)
    for axis_at, shards_of in cuts:
        steps = jnp.exp(jax.random.uniform(jax.random.fold_in(own, axis_at), (shards_of,), jnp.float32, smallest / len(cuts), largest / len(cuts)))
        factor_of = factor_of * jnp.repeat(steps, dims[axis_at] // shards_of).reshape([-1 if axis == axis_at else 1 for axis in range(len(dims))])
    return factor_of


def gaussian(key, dims, width, limit, shards=(), kind=jnp.bfloat16):
    values = width * jax.random.normal(key, dims, jnp.float32)
    if shards:
        values = values * levels(key, dims, shards, -0.22, 0.18)
    return jnp.clip(values, -limit, limit).astype(kind)


def setup_inputs(seed: int = 0) -> dict:
    seeds = jax.random.split(jax.random.key(seed), 8)
    return {
        "hidden_in": gaussian(seeds[0], (TOKENS, D), 1.0, 6.0, ((0, 64), (1, 4))),
        "sender_cache": gaussian(seeds[1], (TOKENS, SK), 1.0, 6.0, ((0, 64), (1, 4))),
        "block_slot": jax.random.permutation(seeds[2], SPANS).astype(jnp.int32),
        "norm_gain": jnp.clip(1.0 + 0.18 * jax.random.normal(seeds[3], (D,), jnp.float32), 0.1, 1.9),
        "kv_weight": gaussian(seeds[4], (D, 2, KV), D ** -0.5, 0.0625, ((0, 32), (2, 4))),
        "proj_in": gaussian(seeds[5], (SK, F), SK ** -0.5, 0.125, ((0, 64), (1, 4))),
        "proj_out": gaussian(seeds[6], (F, 2, KV), F ** -0.5, 0.125, ((0, 256),)),
    }


THETA_BASE = 500000.0

def rotate(keys, positions):
    half = keys.shape[-1] // 2
    freqs = THETA_BASE ** (-(jnp.arange(half, dtype=jnp.float32) * 2.0 / keys.shape[-1]))
    angles = positions.astype(jnp.float32)[:, None] * freqs[None, :]
    cosine = jnp.cos(angles)[:, None, :]
    sine = jnp.sin(angles)[:, None, :]
    first = keys[..., :half]
    second = keys[..., half:]
    return jnp.concatenate([first * cosine - second * sine, second * cosine + first * sine], axis=-1)

def reference(hidden_in, sender_cache, block_slot, norm_gain, kv_weight, proj_in, proj_out):
    rows_total = hidden_in.shape[0]
    blocks = rows_total // TOK_DEV
    inv_root = 1.0 / jnp.sqrt(jnp.float32(rows_total))
    hidden_blocks = hidden_in.reshape(blocks, TOK_DEV, D)
    cache_blocks = sender_cache.reshape(blocks, TOK_DEV, SK)
    kv_flat = kv_weight.reshape(D, 2 * KV)
    out_flat = proj_out.reshape(F, 2 * KV)

    def step(carry, inputs):
        grad_in, grad_out = carry
        block_index, hidden, cache = inputs
        slot = block_slot[block_index // N_DP]
        positions = slot * TOK_DEV + jnp.arange(TOK_DEV, dtype=jnp.int32)
        wide = hidden.astype(jnp.float32)
        mean_sq = lax.optimization_barrier(jnp.mean(wide * wide, axis=1, keepdims=True))
        normed = (wide * lax.rsqrt(mean_sq + 1e-05) * norm_gain[None, :]).astype(jnp.bfloat16)
        kvp = jnp.dot(normed, kv_flat, preferred_element_type=jnp.float32).reshape(TOK_DEV, 2, KV)
        keys = rotate(kvp[:, 0].reshape(TOK_DEV, KV // HD, HD), positions).reshape(TOK_DEV, KV)
        target = jnp.stack([keys, kvp[:, 1]], axis=1).astype(jnp.bfloat16)
        pre = jnp.dot(cache, proj_in, preferred_element_type=jnp.float32)
        act = jax.nn.silu(pre).astype(jnp.bfloat16)
        pred = jnp.dot(act, out_flat, preferred_element_type=jnp.float32).reshape(TOK_DEV, 2, KV)
        err = ((pred - target.astype(jnp.float32)) * inv_root).astype(jnp.bfloat16).reshape(TOK_DEV, 2 * KV)
        back = jnp.dot(err, out_flat.T, preferred_element_type=jnp.float32)
        sig = jax.nn.sigmoid(pre)
        dpre = (back * sig * (1.0 + pre * (1.0 - sig))).astype(jnp.bfloat16)
        grad_out = grad_out + jnp.dot(act.T, err, preferred_element_type=jnp.float32)
        grad_in = grad_in + jnp.dot(cache.T, dpre, preferred_element_type=jnp.float32)
        return ((grad_in, grad_out), None)
    start = (jnp.zeros((SK, F), jnp.float32), jnp.zeros((F, 2 * KV), jnp.float32))
    (grad_in, grad_out), _ = lax.scan(step, start, (jnp.arange(blocks, dtype=jnp.int32), hidden_blocks, cache_blocks))
    return (grad_in, grad_out.reshape(F, 2, KV))
```

```python
import functools

import jax
import jax.numpy as jnp
from jax import lax
from jax.experimental import pallas as pl
from jax.experimental.pallas import tpu as pltpu
from jax.sharding import Mesh
from jax.sharding import PartitionSpec as P

HD = 128
THETA_BASE = 500000.0
SIZES = {"xl": 2, "c": 2, "z": 8, "y": 4, "xh": 2}


def shift(x, axis, step=1):
    n = SIZES[axis]
    return lax.ppermute(x, axis, [(i, (i + step) % n) for i in range(n)])


def ring_gather(x, axis):
    n = SIZES[axis]
    out = {0: x}
    ahead, behind = x, x
    for d in range(1, n // 2):
        ahead = shift(ahead, axis, -1)
        behind = shift(behind, axis, 1)
        out[d], out[n - d] = ahead, behind
    half = x.shape[0] // 2
    low = shift(ahead[:half], axis, -1)
    high = shift(behind[half:], axis, 1)
    out[n // 2] = (low, high)
    return out


def xor_order(x, dim, tl, tc):
    shape = x.shape
    x = x.reshape(shape[:dim] + (2, 2) + shape[dim + 1 :])
    x = jnp.where(tl == 1, jnp.flip(x, dim), x)
    x = jnp.where(tc == 1, jnp.flip(x, dim + 1), x)
    return x.reshape(shape)


def pair_up(own, xh):
    other = shift(own, "xh")
    return jnp.concatenate(
        [jnp.where(xh == 0, own, other), jnp.where(xh == 0, other, own)], axis=0
    )


def place(buffer, block, row):
    return lax.dynamic_update_slice(buffer, block, (row, 0))


def kv_kernel(table, x_ref, w0, w1, w2a, w2b, w3, out_ref):
    out_ref[...] = jnp.zeros_like(out_ref)

    def part(w_ref, first, base, count):
        def body(i, carry):
            which = table[first + i]
            rows = pl.ds(pl.multiple_of(base + i * 256, 256), 256)
            cols = pl.ds(pl.multiple_of((which % 8) * 256, 256), 256)
            out_ref[...] += jnp.dot(
                x_ref[which // 8, :, cols], w_ref[rows, :], preferred_element_type=jnp.float32
            )
            return carry

        lax.fori_loop(0, count, body, 0)

    part(w0, 0, 0, 8)
    part(w1, 8, 0, 8)
    part(w3, 24, 0, 8)
    part(w2a, 16, 0, 4)
    part(w2b, 20, 0, 4)


def kv_matmul(table, x, blocks):
    tokens, cols = x.shape[1], blocks[0].shape[1]
    vmem = pl.BlockSpec(memory_space=pltpu.VMEM)
    return pl.pallas_call(
        kv_kernel,
        out_shape=jax.ShapeDtypeStruct((tokens, cols), jnp.float32),
        in_specs=[pl.BlockSpec(memory_space=pltpu.SMEM)] + [vmem] * 6,
        out_specs=vmem,
        compiler_params=pltpu.CompilerParams(vmem_limit_bytes=40 * 1024 * 1024),
        cost_estimate=pl.CostEstimate(
            flops=2 * 512 * 8192 * 512, bytes_accessed=17 * 1024 * 1024, transcendentals=0
        ),
        name="kv_matmul",
    )(table, x, *blocks)


def per_device(hidden_in, sender_cache, block_slot, norm_gain, kv_weight, proj_in, proj_out):
    rows = hidden_in.shape[0]
    tl, tc = lax.axis_index("xl"), lax.axis_index("c")
    z, y, xh = lax.axis_index("z"), lax.axis_index("y"), lax.axis_index("xh")
    tensor = tl * 2 + tc
    bf16, f32 = jnp.bfloat16, jnp.float32
    inv_root = 1.0 / jnp.sqrt(f32(rows * 64))
    zpos = lambda zz: ((zz >> 1) ^ tensor) * 2 + (zz & 1)

    def tensor_gather(own):
        far = shift(own, "xl")
        return [own, shift(own, "c"), far, shift(far, "c")]

    cache = jnp.concatenate(tensor_gather(sender_cache), axis=1)

    pin = pair_up(proj_in, xh)
    pout = xor_order(
        proj_out.reshape(8, 2, 4, 256).transpose(0, 2, 1, 3), 1, tl, tc
    ).reshape(8, 2048)
    pout = pair_up(pout, xh)

    def gather_yz(block, rel):
        m = block.shape[0]
        near = jnp.zeros((4 * m, block.shape[1]), bf16)
        for d, piece in ring_gather(block, "y").items():
            yy = (y + d) % 4
            if isinstance(piece, tuple):
                near = place(near, piece[0], yy * m)
                near = place(near, piece[1], yy * m + m // 2)
            else:
                near = place(near, piece, yy * m)
        m = 4 * m
        full = jnp.zeros((8 * m, block.shape[1]), bf16)
        for d, piece in ring_gather(near, "z").items():
            zz = (z + d) % 8
            zz = zpos(zz) if rel else zz
            if isinstance(piece, tuple):
                full = place(full, piece[0], zz * m)
                full = place(full, piece[1], zz * m + m // 2)
            else:
                full = place(full, piece, zz * m)
        return full

    pin_full = gather_yz(pin, True)
    pout_full = gather_yz(pout, False)

    wide = hidden_in.astype(f32)
    square = jnp.sum(wide * wide, axis=1, keepdims=True)
    square = square + shift(square, "c")
    square = square + shift(square, "xl")
    scaled = (wide * norm_gain[None, :]).astype(bf16)
    features = jnp.stack(tensor_gather(scaled), axis=0)
    inv_norm = lax.rsqrt(square / 8192.0 + 1e-05)

    shard = kv_weight.reshape(256, 512)
    zr = ring_gather(shard, "z")
    pieces = []
    for d in range(8):
        pieces += list(zr[d]) if isinstance(zr[d], tuple) else [zr[d]]
    yr = ring_gather(jnp.concatenate(pieces, axis=0), "y")
    blocks = [yr[0], yr[1], yr[2][0], yr[2][1], yr[3]]
    dd = jnp.arange(32, dtype=jnp.int32)
    zz = (z + dd % 8) % 8
    yy = (y + dd // 8) % 4
    table = ((zz >> 1) ^ tensor) * 8 + (zz & 1) * 4 + yy
    kv = kv_matmul(table, features, blocks) * inv_norm

    half = HD // 2
    freqs = THETA_BASE ** (-(jnp.arange(half, dtype=f32) * 2.0 / HD))
    positions = block_slot[0] * rows + jnp.arange(rows, dtype=jnp.int32)
    angles = positions.astype(f32)[:, None] * freqs[None, :]
    cosine, sine = jnp.cos(angles), jnp.sin(angles)
    heads = []
    for h in range(2):
        a = kv[:, h * HD : h * HD + half]
        b = kv[:, h * HD + half : (h + 1) * HD]
        heads += [a * cosine - b * sine, b * cosine + a * sine]
    target = jnp.concatenate(heads + [kv[:, 256:]], axis=1).astype(bf16)

    pre = jnp.dot(cache, pin_full, preferred_element_type=f32)
    act = jax.nn.silu(pre).astype(bf16)
    partial = jnp.dot(act, pout_full, preferred_element_type=f32).reshape(rows, 4, 512)
    odd = shift(jnp.concatenate([partial[:, 1], partial[:, 3]], axis=1).astype(bf16), "c")
    mine = partial[:, 0] + odd[:, :512].astype(f32)
    far = partial[:, 2] + odd[:, 512:].astype(f32)
    pred = mine + shift(far.astype(bf16), "xl").astype(f32)
    err = ((pred - target.astype(f32)) * inv_root).astype(bf16)
    err_full = jnp.concatenate(tensor_gather(err), axis=1)

    contract_rows = (((0,), (0,)), ((), ()))
    gout = lax.dot_general(act, err_full, contract_rows, preferred_element_type=f32).astype(bf16)
    back = lax.dot_general(
        err_full, pout_full, (((1,), (1,)), ((), ())), preferred_element_type=f32
    )
    sig = jax.nn.sigmoid(pre)
    dpre = (back * sig * (1.0 + pre * (1.0 - sig))).astype(bf16)
    gin = lax.dot_general(cache, dpre, contract_rows, preferred_element_type=f32).astype(bf16)

    def sum_y(g):
        def part(at):
            return lax.dynamic_slice_in_dim(g, at % 4, 1, axis=1)[:, 0]

        total = part(y).astype(f32)
        for e in (1, 3, 2):
            total = total + shift(part(y + e), "y", e).astype(f32)
        return total

    def sum_xh(g):
        keep = jnp.where(xh == 0, g[:, 0], g[:, 1]).astype(f32)
        give = jnp.where(xh == 0, g[:, 1], g[:, 0])
        return keep + shift(give, "xh").astype(f32)

    go = sum_y(gout.reshape(8, 4, 16, 2048)).astype(bf16)
    go = sum_xh(go.reshape(8, 2, 8, 2048)).astype(bf16)
    gi = sum_xh(gin.reshape(32, 2, 32, 512)).astype(bf16)
    gi = sum_y(gi.reshape(8, 4, 32, 512)).astype(bf16)
    gi = xor_order(gi.reshape(4, 2, 32, 512), 0, tl, tc).reshape(8, 32, 512)
    go = go.reshape(8, 8, 4, 512).transpose(0, 2, 1, 3).reshape(8, 32, 512)
    both = lax.all_to_all(jnp.concatenate([gi, go], axis=1), "z", 0, 0)
    both = jnp.sum(both.astype(f32), axis=0)
    grad_in = both[:32]
    grad_out = xor_order(both[32:].reshape(4, 8, 512), 0, tl, tc)
    grad_out = grad_out.reshape(4, 8, 2, 256).transpose(1, 2, 0, 3).reshape(8, 2, 1024)
    return grad_in, grad_out


def solution(mesh):
    names = ("xl", "c", "z", "y", "xh")
    fine = Mesh(mesh.devices.reshape(tuple(SIZES[n] for n in names)), names)
    tensor, token, dp = ("xl", "c"), ("z", "y"), ("xh",)
    placed = (
        P(token + dp, tensor),
        P(token + dp, tensor),
        P(token),
        P(tensor),
        P(token, None, tensor),
        P(token + dp, tensor),
        P(tensor + token + dp, None, None),
    )
    return jax.shard_map(
        per_device,
        mesh=fine,
        in_specs=placed,
        out_specs=(P(token + dp, tensor), P(tensor + token + dp, None, None)),
        check_vma=False,
    )
```

```python
import jax
import jax.numpy as jnp
from jax import lax
from jax.sharding import Mesh
from jax.sharding import PartitionSpec as P

HD = 128
THETA_BASE = 500000.0
SIZES = {"xl": 2, "c": 2, "z": 8, "y": 4, "xh": 2}


def shift(x, axis, step=1):
    n = SIZES[axis]
    return lax.ppermute(x, axis, [(i, (i + step) % n) for i in range(n)])


def ring_gather(x, axis):
    n = SIZES[axis]
    out = {0: x}
    ahead, behind = x, x
    for d in range(1, n // 2):
        ahead = shift(ahead, axis, -1)
        behind = shift(behind, axis, 1)
        out[d], out[n - d] = ahead, behind
    half = x.shape[0] // 2
    low = shift(ahead[:half], axis, -1)
    high = shift(behind[half:], axis, 1)
    out[n // 2] = (low, high)
    return out


def xor_order(x, dim, tl, tc):
    shape = x.shape
    x = x.reshape(shape[:dim] + (2, 2) + shape[dim + 1 :])
    x = jnp.where(tl == 1, jnp.flip(x, dim), x)
    x = jnp.where(tc == 1, jnp.flip(x, dim + 1), x)
    return x.reshape(shape)


def place(buffer, block, *at):
    return lax.dynamic_update_slice(buffer, block, at)


def per_device(hidden_in, sender_cache, block_slot, norm_gain, kv_weight, proj_in, proj_out):
    rows = hidden_in.shape[0]
    tl, tc = lax.axis_index("xl"), lax.axis_index("c")
    z, y, xh = lax.axis_index("z"), lax.axis_index("y"), lax.axis_index("xh")
    tensor = tl * 2 + tc
    bf16, f32 = jnp.bfloat16, jnp.float32
    inv_root = 1.0 / jnp.sqrt(f32(rows * 64))
    zpos = lambda zz: ((zz >> 1) ^ tensor) * 2 + (zz & 1)

    def tensor_gather(own):
        far = shift(own, "xl")
        return [own, shift(own, "c"), far, shift(far, "c")]

    pout = xor_order(proj_out.reshape(8, 2, 4, 256).transpose(2, 0, 1, 3), 0, tl, tc)
    own = jnp.concatenate([proj_in, pout.reshape(32, 512)], axis=0)
    other = shift(own, "xh")
    pair = jnp.stack([jnp.where(xh == 0, own, other), jnp.where(xh == 0, other, own)])
    pair_in = pair[:, :32].reshape(64, 512)
    pair_out = pair[:, 32:].reshape(2, 4, 8, 512).transpose(1, 0, 2, 3).reshape(64, 512)
    near_in = jnp.zeros((256, 512), bf16)
    near_out = jnp.zeros((4, 64, 512), bf16)
    for d, piece in ring_gather(jnp.concatenate([pair_in, pair_out], axis=0), "y").items():
        yy = (y + d) % 4
        first, second = piece if isinstance(piece, tuple) else (piece[:64], piece[64:])
        near_in = place(near_in, first, yy * 64, 0)
        near_out = place(near_out, second.reshape(4, 16, 512), 0, yy * 16, 0)
    pin_full = jnp.zeros((2048, 512), bf16)
    pout_full = jnp.zeros((4, 512, 512), bf16)
    payload = jnp.concatenate([near_in, near_out.reshape(256, 512)], axis=0)
    for d, piece in ring_gather(payload, "z").items():
        zz = (z + d) % 8
        first, second = piece if isinstance(piece, tuple) else (piece[:256], piece[256:])
        pin_full = place(pin_full, first, zpos(zz) * 256, 0)
        pout_full = place(pout_full, second.reshape(4, 64, 512), 0, zz * 64, 0)

    weight = lax.all_gather(kv_weight.reshape(256, 512), ("z", "y"), axis=0, tiled=True)

    cache = jnp.concatenate(tensor_gather(sender_cache), axis=1)
    wide = hidden_in.astype(f32)
    square = jnp.sum(wide * wide, axis=1, keepdims=True)
    square = square + shift(square, "c")
    square = square + shift(square, "xl")
    scaled = (wide * norm_gain[None, :]).astype(bf16)
    scaled, cache = lax.optimization_barrier((scaled, cache))
    features = tensor_gather(scaled)
    inv_norm = lax.rsqrt(square / 8192.0 + 1e-05)
    kv = jnp.zeros((rows, 512), f32)
    for r in range(4):
        block = lax.dynamic_slice_in_dim(weight, (tensor ^ r) * 2048, 2048, axis=0)
        kv = kv + jnp.dot(features[r], block, preferred_element_type=f32)
    kv = kv * inv_norm

    half = HD // 2
    freqs = THETA_BASE ** (-(jnp.arange(half, dtype=f32) * 2.0 / HD))
    positions = block_slot[0] * rows + jnp.arange(rows, dtype=jnp.int32)
    angles = positions.astype(f32)[:, None] * freqs[None, :]
    cosine, sine = jnp.cos(angles), jnp.sin(angles)
    heads = []
    for h in range(2):
        a = kv[:, h * HD : h * HD + half]
        b = kv[:, h * HD + half : (h + 1) * HD]
        heads += [a * cosine - b * sine, b * cosine + a * sine]
    target = jnp.concatenate(heads + [kv[:, 256:]], axis=1).astype(bf16)

    pre = jnp.dot(cache, pin_full, preferred_element_type=f32)
    act = jax.nn.silu(pre).astype(bf16)
    partial = [jnp.dot(act, pout_full[r], preferred_element_type=f32) for r in range(4)]
    odd = shift(jnp.concatenate([partial[1], partial[3]], axis=1).astype(bf16), "c")
    mine = partial[0] + odd[:, :512].astype(f32)
    far = partial[2] + odd[:, 512:].astype(f32)
    pred = mine + shift(far.astype(bf16), "xl").astype(f32)
    err = ((pred - target.astype(f32)) * inv_root).astype(bf16)
    errs = tensor_gather(err)

    contract_rows = (((0,), (0,)), ((), ()))
    gout = [
        lax.dot_general(act, e, contract_rows, preferred_element_type=f32).astype(bf16)
        for e in errs
    ]
    gout = jnp.concatenate(gout, axis=1)
    back = sum(
        lax.dot_general(
            errs[r], pout_full[r], (((1,), (1,)), ((), ())), preferred_element_type=f32
        )
        for r in range(4)
    )
    sig = jax.nn.sigmoid(pre)
    dpre = (back * sig * (1.0 + pre * (1.0 - sig))).astype(bf16)
    gin = lax.dot_general(cache, dpre, contract_rows, preferred_element_type=f32).astype(bf16)

    def sum_y(g):
        def part(at):
            return lax.dynamic_slice_in_dim(g, at % 4, 1, axis=1)[:, 0]

        total = part(y).astype(f32)
        for e in (1, 3, 2):
            total = total + shift(part(y + e), "y", e).astype(f32)
        return total

    def sum_xh(g):
        keep = jnp.where(xh == 0, g[:, 0], g[:, 1]).astype(f32)
        give = jnp.where(xh == 0, g[:, 1], g[:, 0])
        return keep + shift(give, "xh").astype(f32)

    go = sum_y(gout.reshape(8, 4, 16, 2048)).astype(bf16)
    go = sum_xh(go.reshape(8, 2, 8, 2048)).astype(bf16)
    gi = sum_xh(gin.reshape(32, 2, 32, 512)).astype(bf16)
    gi = sum_y(gi.reshape(8, 4, 32, 512)).astype(bf16)
    gi = xor_order(gi.reshape(4, 2, 32, 512), 0, tl, tc).reshape(8, 32, 512)
    go = go.reshape(8, 8, 4, 512).transpose(0, 2, 1, 3).reshape(8, 32, 512)
    both = lax.all_to_all(jnp.concatenate([gi, go], axis=1), "z", 0, 0)
    both = jnp.sum(both.astype(f32), axis=0)
    grad_in = both[:32]
    grad_out = xor_order(both[32:].reshape(4, 8, 512), 0, tl, tc)
    grad_out = grad_out.reshape(4, 8, 2, 256).transpose(1, 2, 0, 3).reshape(8, 2, 1024)
    return grad_in, grad_out


def solution(mesh):
    names = ("xl", "c", "z", "y", "xh")
    fine = Mesh(mesh.devices.reshape(tuple(SIZES[n] for n in names)), names)
    tensor, token, dp = ("xl", "c"), ("z", "y"), ("xh",)
    placed = (
        P(token + dp, tensor),
        P(token + dp, tensor),
        P(token),
        P(tensor),
        P(token, None, tensor),
        P(token + dp, tensor),
        P(tensor + token + dp, None, None),
    )
    return jax.shard_map(
        per_device,
        mesh=fine,
        in_specs=placed,
        out_specs=(P(token + dp, tensor), P(tensor + token + dp, None, None)),
        check_vma=False,
    )
```

```python
import jax
import jax.numpy as jnp
from jax import lax
from jax.experimental import pallas as pl
from jax.experimental.pallas import tpu as pltpu
from jax.sharding import Mesh
from jax.sharding import PartitionSpec as P

HD = 128
THETA_BASE = 500000.0
SIZES = {"xl": 2, "c": 2, "z": 8, "y": 4, "xh": 2}


def shift(x, axis, step=1):
    n = SIZES[axis]
    return lax.ppermute(x, axis, [(i, (i + step) % n) for i in range(n)])


def ring_gather(x, axis):
    n = SIZES[axis]
    out = {0: x}
    ahead, behind = x, x
    for d in range(1, n // 2):
        ahead = shift(ahead, axis, -1)
        behind = shift(behind, axis, 1)
        out[d], out[n - d] = ahead, behind
    half = x.shape[0] // 2
    low = shift(ahead[:half], axis, -1)
    high = shift(behind[half:], axis, 1)
    out[n // 2] = (low, high)
    return out


def xor_order(x, dim, tl, tc):
    shape = x.shape
    x = x.reshape(shape[:dim] + (2, 2) + shape[dim + 1 :])
    x = jnp.where(tl == 1, jnp.flip(x, dim), x)
    x = jnp.where(tc == 1, jnp.flip(x, dim + 1), x)
    return x.reshape(shape)


def place(buffer, block, *at):
    return lax.dynamic_update_slice(buffer, block, at)


def target_kernel(table, w_ref, *refs):
    x_refs, (norm_ref, cos_ref, sin_ref, out_ref) = refs[:4], refs[4:8]
    x_buf, w_buf, acc, sems = refs[8:]
    sources = [x.at[:, h * 1024 : (h + 1) * 1024] for x in x_refs for h in range(2)]
    copies = []
    for i in range(8):
        first = table[i // 2] * 8 + (i % 2) * 4
        x = pltpu.make_async_copy(sources[i], x_buf.at[i], sems.at[0, i])
        w = pltpu.make_async_copy(w_ref.at[pl.ds(first, 4)], w_buf.at[i], sems.at[1, i])
        x.start()
        w.start()
        copies.append((x, w))
    for i, (x, w) in enumerate(copies):
        x.wait()
        w.wait()
        for p in range(2):
            product = jnp.dot(
                x_buf[i],
                w_buf[i, :, p * 256 : (p + 1) * 256].reshape(1024, 256),
                preferred_element_type=jnp.float32,
            )
            acc[p] = product if i == 0 else acc[p] + product
    for p in range(2):
        kv = acc[p] * norm_ref[...]
        for h in range(2):
            head = kv[:, h * HD : (h + 1) * HD]
            if p == 0:
                head = head * cos_ref[...] + pltpu.roll(head, HD // 2, 1) * sin_ref[...]
            cols = slice(p * 256 + h * HD, p * 256 + (h + 1) * HD)
            out_ref[:, cols] = head.astype(jnp.bfloat16)


def targets(table, weight, x, inv_norm, cosine, sine):
    vmem = pl.BlockSpec(memory_space=pltpu.VMEM)
    hbm = pl.BlockSpec(memory_space=pl.ANY)
    return pl.pallas_call(
        target_kernel,
        out_shape=jax.ShapeDtypeStruct((512, 512), jnp.bfloat16),
        in_specs=[pl.BlockSpec(memory_space=pltpu.SMEM)] + [hbm] * 5 + [vmem] * 3,
        out_specs=vmem,
        scratch_shapes=[
            pltpu.VMEM((8, 512, 1024), jnp.bfloat16),
            pltpu.VMEM((8, 4, 512, 256), jnp.bfloat16),
            pltpu.VMEM((2, 512, 256), jnp.float32),
            pltpu.SemaphoreType.DMA((2, 8)),
        ],
        compiler_params=pltpu.CompilerParams(vmem_limit_bytes=56 * 1024 * 1024),
        cost_estimate=pl.CostEstimate(
            flops=2 * 512 * 512 * 8192, bytes_accessed=18 * 1024 * 1024, transcendentals=0
        ),
        name="targets",
    )(table, weight, *x, inv_norm, cosine, sine)


def per_device(hidden_in, sender_cache, block_slot, norm_gain, kv_weight, proj_in, proj_out):
    rows = hidden_in.shape[0]
    tl, tc = lax.axis_index("xl"), lax.axis_index("c")
    z, y, xh = lax.axis_index("z"), lax.axis_index("y"), lax.axis_index("xh")
    tensor = tl * 2 + tc
    bf16, f32 = jnp.bfloat16, jnp.float32
    inv_root = 1.0 / jnp.sqrt(f32(rows * 64))
    zpos = lambda zz: ((zz >> 1) ^ tensor) * 2 + (zz & 1)

    def tensor_gather(own):
        far = shift(own, "xl")
        return [own, shift(own, "c"), far, shift(far, "c")]

    pout = xor_order(proj_out.reshape(8, 2, 4, 256).transpose(2, 0, 1, 3), 0, tl, tc)
    own = jnp.concatenate([proj_in, pout.reshape(32, 512)], axis=0)
    other = shift(own, "xh")
    pair = jnp.stack([jnp.where(xh == 0, own, other), jnp.where(xh == 0, other, own)])
    pair_in = pair[:, :32].reshape(64, 512)
    pair_out = pair[:, 32:].reshape(2, 4, 8, 512).transpose(1, 0, 2, 3).reshape(64, 512)
    near_in = jnp.zeros((256, 512), bf16)
    near_out = jnp.zeros((4, 64, 512), bf16)
    for d, piece in ring_gather(jnp.concatenate([pair_in, pair_out], axis=0), "y").items():
        yy = (y + d) % 4
        first, second = piece if isinstance(piece, tuple) else (piece[:64], piece[64:])
        near_in = place(near_in, first, yy * 64, 0)
        near_out = place(near_out, second.reshape(4, 16, 512), 0, yy * 16, 0)
    pin_full = jnp.zeros((2048, 512), bf16)
    pout_full = jnp.zeros((4, 512, 512), bf16)
    payload = jnp.concatenate([near_in, near_out.reshape(256, 512)], axis=0)
    for d, piece in ring_gather(payload, "z").items():
        zz = (z + d) % 8
        first, second = piece if isinstance(piece, tuple) else (piece[:256], piece[256:])
        pin_full = place(pin_full, first, zpos(zz) * 256, 0)
        pout_full = place(pout_full, second.reshape(4, 64, 512), 0, zz * 64, 0)

    shard = kv_weight.transpose(1, 0, 2).reshape(512, 256)
    weight = lax.all_gather(shard, ("z", "y"), axis=0, tiled=True).reshape(32, 512, 256)

    cache = jnp.concatenate(tensor_gather(sender_cache), axis=1)
    wide = hidden_in.astype(f32)
    square = jnp.sum(wide * wide, axis=1, keepdims=True)
    square = square + shift(square, "c")
    square = square + shift(square, "xl")
    scaled = (wide * norm_gain[None, :]).astype(bf16)
    scaled, cache = lax.optimization_barrier((scaled, cache))
    features = tensor_gather(scaled)
    inv_norm = lax.rsqrt(square / 8192.0 + 1e-05)
    half = HD // 2
    freqs = THETA_BASE ** (-(jnp.arange(half, dtype=f32) * 2.0 / HD))
    positions = block_slot[0] * rows + jnp.arange(rows, dtype=jnp.int32)
    angles = positions.astype(f32)[:, None] * freqs[None, :]
    cosine, sine = jnp.cos(angles), jnp.sin(angles)
    cosine = jnp.concatenate([cosine, cosine], axis=1)
    sine = jnp.concatenate([-sine, sine], axis=1)
    table = tensor ^ jnp.arange(4, dtype=jnp.int32)
    target = targets(table, weight, features, inv_norm, cosine, sine)

    pre = jnp.dot(cache, pin_full, preferred_element_type=f32)
    act = jax.nn.silu(pre).astype(bf16)
    partial = [jnp.dot(act, pout_full[r], preferred_element_type=f32) for r in range(4)]
    odd = shift(jnp.concatenate([partial[1], partial[3]], axis=1).astype(bf16), "c")
    mine = partial[0] + odd[:, :512].astype(f32)
    far = partial[2] + odd[:, 512:].astype(f32)
    pred = mine + shift(far.astype(bf16), "xl").astype(f32)
    err = ((pred - target.astype(f32)) * inv_root).astype(bf16)
    errs = tensor_gather(err)
    theirs, *errs = lax.optimization_barrier((sender_cache, *errs))

    contract_rows = (((0,), (0,)), ((), ()))
    contract_cols = (((1,), (1,)), ((), ()))

    def exchange(g, axis):
        return jnp.sum(lax.all_to_all(g, axis, 0, 0).astype(f32), axis=0)

    def exchange_y(g):
        def part(at):
            return lax.dynamic_slice_in_dim(g, at % 4, 1, axis=1)[:, 0]

        total = part(y).astype(f32)
        for e in (1, 3, 2):
            total = total + shift(part(y + e), "y", e).astype(f32)
        return total

    def half_columns(x, which):
        unit = jnp.arange(256, dtype=jnp.int32)
        source = unit // 32 * 64 + which * 32 + unit % 32
        chosen = jnp.arange(512, dtype=jnp.int32)[:, None] == source[None, :]
        return jnp.dot(x, chosen.astype(bf16), preferred_element_type=f32).astype(bf16)

    back = sum(
        lax.dot_general(errs[r], pout_full[r], contract_cols, preferred_element_type=f32)
        for r in range(4)
    )
    sig = jax.nn.sigmoid(pre)
    dpre = (back * sig * (1.0 + pre * (1.0 - sig))).astype(bf16)
    (dpre,) = lax.optimization_barrier((dpre,))
    their_dpre = shift(dpre, "xh")
    theirs = tensor_gather(shift(half_columns(theirs, 1 - xh), "xh"))
    theirs = jnp.concatenate(theirs, axis=1)
    ours = [half_columns(cache[:, r * 512 : (r + 1) * 512], xh) for r in range(4)]
    ours = jnp.concatenate(ours, axis=1)
    go = lax.dot_general(
        act, jnp.concatenate(errs, axis=1), contract_rows, preferred_element_type=f32
    )
    go = exchange_y(go.astype(bf16).reshape(8, 4, 16, 2048)).astype(bf16)
    gi = lax.dot_general(ours, dpre, contract_rows, preferred_element_type=f32)
    gi = gi + lax.dot_general(theirs, their_dpre, contract_rows, preferred_element_type=f32)
    gi = gi.astype(bf16).reshape(4, 2, 128, 512)
    gi = xor_order(gi, 0, tl, tc).reshape(8, 128, 512)
    first = exchange(gi[:, :, :256], "z").astype(bf16)
    second = exchange_y(gi[:, :, 256:].reshape(8, 4, 32, 256)).astype(bf16)
    go = go.reshape(8, 2, 8, 2048)
    keep = lax.dynamic_slice_in_dim(go, xh, 1, axis=1)[:, 0]
    give = lax.dynamic_slice_in_dim(go, 1 - xh, 1, axis=1)[:, 0]
    go = (keep.astype(f32) + shift(give, "xh").astype(f32)).astype(bf16)
    first, go = lax.optimization_barrier((first, go))
    first = exchange_y(first.reshape(1, 4, 32, 256))[0]
    last = exchange(jnp.concatenate([second, go.reshape(8, 64, 256)], axis=1), "z")
    grad_in = jnp.concatenate([first, last[:32]], axis=1)
    grad_out = xor_order(last[32:].reshape(8, 4, 2, 256), 1, tl, tc)
    grad_out = grad_out.transpose(0, 2, 1, 3).reshape(8, 2, 1024)
    return grad_in, grad_out


def solution(mesh):
    names = ("xl", "c", "z", "y", "xh")
    fine = Mesh(mesh.devices.reshape(tuple(SIZES[n] for n in names)), names)
    tensor, token, dp = ("xl", "c"), ("z", "y"), ("xh",)
    placed = (
        P(token + dp, tensor),
        P(token + dp, tensor),
        P(token),
        P(tensor),
        P(token, None, tensor),
        P(token + dp, tensor),
        P(tensor + token + dp, None, None),
    )
    return jax.shard_map(
        per_device,
        mesh=fine,
        in_specs=placed,
        out_specs=(P(token + dp, tensor), P(tensor + token + dp, None, None)),
        check_vma=False,
    )
```

```python
import jax
import jax.numpy as jnp
from jax import lax
from jax.experimental import pallas as pl
from jax.experimental.pallas import tpu as pltpu
from jax.sharding import Mesh
from jax.sharding import PartitionSpec as P

HD = 128
THETA_BASE = 500000.0
SIZES = {"xl": 2, "c": 2, "z": 8, "y": 4, "xh": 2}


def shift(x, axis, step=1):
    n = SIZES[axis]
    return lax.ppermute(x, axis, [(i, (i + step) % n) for i in range(n)])


def ring_gather(x, axis):
    n = SIZES[axis]
    out = {0: x}
    ahead, behind = x, x
    for d in range(1, n // 2):
        ahead = shift(ahead, axis, -1)
        behind = shift(behind, axis, 1)
        out[d], out[n - d] = ahead, behind
    half = x.shape[0] // 2
    low = shift(ahead[:half], axis, -1)
    high = shift(behind[half:], axis, 1)
    out[n // 2] = (low, high)
    return out


def xor_order(x, dim, tl, tc):
    shape = x.shape
    x = x.reshape(shape[:dim] + (2, 2) + shape[dim + 1 :])
    x = jnp.where(tl == 1, jnp.flip(x, dim), x)
    x = jnp.where(tc == 1, jnp.flip(x, dim + 1), x)
    return x.reshape(shape)


def place(buffer, block, *at):
    return lax.dynamic_update_slice(buffer, block, at)


def target_kernel(table, w_ref, *refs):
    x_refs, (norm_ref, cos_ref, sin_ref, out_ref) = refs[:4], refs[4:8]
    x_buf, w_buf, acc, sems = refs[8:]
    sources = [x.at[:, h * 1024 : (h + 1) * 1024] for x in x_refs for h in range(2)]
    copies = []
    for i in range(8):
        first = table[i // 2] * 8 + (i % 2) * 4
        x = pltpu.make_async_copy(sources[i], x_buf.at[i], sems.at[0, i])
        w = pltpu.make_async_copy(w_ref.at[pl.ds(first, 4)], w_buf.at[i], sems.at[1, i])
        x.start()
        w.start()
        copies.append((x, w))
    for i, (x, w) in enumerate(copies):
        x.wait()
        w.wait()
        for p in range(2):
            product = jnp.dot(
                x_buf[i],
                w_buf[i, :, p * 256 : (p + 1) * 256].reshape(1024, 256),
                preferred_element_type=jnp.float32,
            )
            acc[p] = product if i == 0 else acc[p] + product
    for p in range(2):
        kv = acc[p] * norm_ref[...]
        for h in range(2):
            head = kv[:, h * HD : (h + 1) * HD]
            if p == 0:
                head = head * cos_ref[...] + pltpu.roll(head, HD // 2, 1) * sin_ref[...]
            cols = slice(p * 256 + h * HD, p * 256 + (h + 1) * HD)
            out_ref[:, cols] = head.astype(jnp.bfloat16)


def targets(table, weight, x, inv_norm, cosine, sine):
    vmem = pl.BlockSpec(memory_space=pltpu.VMEM)
    hbm = pl.BlockSpec(memory_space=pl.ANY)
    return pl.pallas_call(
        target_kernel,
        out_shape=jax.ShapeDtypeStruct((512, 512), jnp.bfloat16),
        in_specs=[pl.BlockSpec(memory_space=pltpu.SMEM)] + [hbm] * 5 + [vmem] * 3,
        out_specs=vmem,
        scratch_shapes=[
            pltpu.VMEM((8, 512, 1024), jnp.bfloat16),
            pltpu.VMEM((8, 4, 512, 256), jnp.bfloat16),
            pltpu.VMEM((2, 512, 256), jnp.float32),
            pltpu.SemaphoreType.DMA((2, 8)),
        ],
        compiler_params=pltpu.CompilerParams(vmem_limit_bytes=56 * 1024 * 1024),
        cost_estimate=pl.CostEstimate(
            flops=2 * 512 * 512 * 8192, bytes_accessed=18 * 1024 * 1024, transcendentals=0
        ),
        name="targets",
    )(table, weight, *x, inv_norm, cosine, sine)


def per_device(hidden_in, sender_cache, block_slot, norm_gain, kv_weight, proj_in, proj_out):
    rows = hidden_in.shape[0]
    tl, tc = lax.axis_index("xl"), lax.axis_index("c")
    z, y, xh = lax.axis_index("z"), lax.axis_index("y"), lax.axis_index("xh")
    tensor = tl * 2 + tc
    bf16, f32 = jnp.bfloat16, jnp.float32
    inv_root = 1.0 / jnp.sqrt(f32(rows * 64))
    zpos = lambda zz: ((zz >> 1) ^ tensor) * 2 + (zz & 1)

    def tensor_gather(own):
        far = shift(own, "xl")
        return [own, shift(own, "c"), far, shift(far, "c")]

    pout = xor_order(proj_out.reshape(8, 2, 4, 256).transpose(2, 0, 1, 3), 0, tl, tc)
    own = jnp.concatenate([proj_in, pout.reshape(32, 512)], axis=0)
    other = shift(own, "xh")
    pair = jnp.stack([jnp.where(xh == 0, own, other), jnp.where(xh == 0, other, own)])
    pair_in = pair[:, :32].reshape(64, 512)
    pair_out = pair[:, 32:].reshape(2, 4, 8, 512).transpose(1, 0, 2, 3).reshape(64, 512)
    near_in = jnp.zeros((256, 512), bf16)
    near_out = jnp.zeros((4, 64, 512), bf16)
    for d, piece in ring_gather(jnp.concatenate([pair_in, pair_out], axis=0), "y").items():
        yy = (y + d) % 4
        first, second = piece if isinstance(piece, tuple) else (piece[:64], piece[64:])
        near_in = place(near_in, first, yy * 64, 0)
        near_out = place(near_out, second.reshape(4, 16, 512), 0, yy * 16, 0)
    pin_full = jnp.zeros((2048, 512), bf16)
    pout_full = jnp.zeros((4, 512, 512), bf16)
    payload = jnp.concatenate([near_in, near_out.reshape(256, 512)], axis=0)
    for d, piece in ring_gather(payload, "z").items():
        zz = (z + d) % 8
        first, second = piece if isinstance(piece, tuple) else (piece[:256], piece[256:])
        pin_full = place(pin_full, first, zpos(zz) * 256, 0)
        pout_full = place(pout_full, second.reshape(4, 64, 512), 0, zz * 64, 0)

    shard = kv_weight.transpose(1, 0, 2).reshape(512, 256)
    weight = lax.all_gather(shard, ("z", "y"), axis=0, tiled=True).reshape(32, 512, 256)

    cache = jnp.concatenate(tensor_gather(sender_cache), axis=1)
    wide = hidden_in.astype(f32)
    square = jnp.sum(wide * wide, axis=1, keepdims=True)
    square = square + shift(square, "c")
    square = square + shift(square, "xl")
    scaled = (wide * norm_gain[None, :]).astype(bf16)
    scaled, cache = lax.optimization_barrier((scaled, cache))
    features = tensor_gather(scaled)
    inv_norm = lax.rsqrt(square / 8192.0 + 1e-05)
    half = HD // 2
    freqs = THETA_BASE ** (-(jnp.arange(half, dtype=f32) * 2.0 / HD))
    positions = block_slot[0] * rows + jnp.arange(rows, dtype=jnp.int32)
    angles = positions.astype(f32)[:, None] * freqs[None, :]
    cosine, sine = jnp.cos(angles), jnp.sin(angles)
    cosine = jnp.concatenate([cosine, cosine], axis=1)
    sine = jnp.concatenate([-sine, sine], axis=1)
    def half_columns(x, which):
        unit = jnp.arange(256, dtype=jnp.int32)
        source = unit // 32 * 64 + which * 32 + unit % 32
        chosen = jnp.arange(512, dtype=jnp.int32)[:, None] == source[None, :]
        return jnp.dot(x, chosen.astype(bf16), preferred_element_type=f32).astype(bf16)

    pre = jnp.dot(cache, pin_full, preferred_element_type=f32)
    act = jax.nn.silu(pre).astype(bf16)
    partial = [jnp.dot(act, pout_full[r], preferred_element_type=f32) for r in range(4)]
    odd = shift(jnp.concatenate([partial[1], partial[3]], axis=1).astype(bf16), "c")
    mine = partial[0] + odd[:, :512].astype(f32)
    away = (partial[2] + odd[:, 512:].astype(f32)).astype(bf16)
    theirs, features[2] = lax.optimization_barrier((sender_cache, features[2]))
    theirs = shift(half_columns(theirs, 1 - xh), "xh")
    away, theirs, features[3] = lax.optimization_barrier((away, theirs, features[3]))
    pred = mine + shift(away, "xl").astype(f32)
    ours = [half_columns(cache[:, r * 512 : (r + 1) * 512], xh) for r in range(4)]
    ours = jnp.concatenate(ours, axis=1)
    pout_flat = pout_full.transpose(1, 0, 2).reshape(512, 2048)
    weight, ours, pout_flat = lax.optimization_barrier((weight, ours, pout_flat))
    table = tensor ^ jnp.arange(4, dtype=jnp.int32)
    target = targets(table, weight, features, inv_norm, cosine, sine)
    err = ((pred - target.astype(f32)) * inv_root).astype(bf16)
    errs = tensor_gather(err)
    theirs, *errs = lax.optimization_barrier((theirs, *errs))

    contract_rows = (((0,), (0,)), ((), ()))
    contract_cols = (((1,), (1,)), ((), ()))

    def exchange(g, axis):
        return jnp.sum(lax.all_to_all(g, axis, 0, 0).astype(f32), axis=0)

    def exchange_y(g):
        def part(at):
            return lax.dynamic_slice_in_dim(g, at % 4, 1, axis=1)[:, 0]

        total = part(y).astype(f32)
        for e in (1, 3, 2):
            total = total + shift(part(y + e), "y", e).astype(f32)
        return total

    err = jnp.concatenate(errs, axis=1)
    back = lax.dot_general(err, pout_flat, contract_cols, preferred_element_type=f32)
    sig = jax.nn.sigmoid(pre)
    dpre = (back * sig * (1.0 + pre * (1.0 - sig))).astype(bf16)
    dpre, err = lax.optimization_barrier((dpre, err))
    their_dpre = shift(dpre, "xh")
    theirs = jnp.concatenate(tensor_gather(theirs), axis=1)
    go = lax.dot_general(act, err, contract_rows, preferred_element_type=f32)
    go = exchange_y(go.astype(bf16).reshape(8, 4, 16, 2048)).astype(bf16)
    gi = lax.dot_general(ours, dpre, contract_rows, preferred_element_type=f32)
    gi = gi + lax.dot_general(theirs, their_dpre, contract_rows, preferred_element_type=f32)
    gi = gi.astype(bf16).reshape(4, 2, 128, 512)
    gi = xor_order(gi, 0, tl, tc).reshape(8, 128, 512)
    first = exchange(gi[:, :, :256], "z").astype(bf16)
    second = exchange_y(gi[:, :, 256:].reshape(8, 4, 32, 256)).astype(bf16)
    go = go.reshape(8, 2, 8, 2048)
    keep = lax.dynamic_slice_in_dim(go, xh, 1, axis=1)[:, 0]
    give = lax.dynamic_slice_in_dim(go, 1 - xh, 1, axis=1)[:, 0]
    go = (keep.astype(f32) + shift(give, "xh").astype(f32)).astype(bf16)
    first, go = lax.optimization_barrier((first, go))
    first = exchange_y(first.reshape(1, 4, 32, 256))[0]
    last = exchange(jnp.concatenate([second, go.reshape(8, 64, 256)], axis=1), "z")
    grad_in = jnp.concatenate([first, last[:32]], axis=1)
    grad_out = xor_order(last[32:].reshape(8, 4, 2, 256), 1, tl, tc)
    grad_out = grad_out.transpose(0, 2, 1, 3).reshape(8, 2, 1024)
    return grad_in, grad_out


def solution(mesh):
    names = ("xl", "c", "z", "y", "xh")
    fine = Mesh(mesh.devices.reshape(tuple(SIZES[n] for n in names)), names)
    tensor, token, dp = ("xl", "c"), ("z", "y"), ("xh",)
    placed = (
        P(token + dp, tensor),
        P(token + dp, tensor),
        P(token),
        P(tensor),
        P(token, None, tensor),
        P(token + dp, tensor),
        P(tensor + token + dp, None, None),
    )
    return jax.shard_map(
        per_device,
        mesh=fine,
        in_specs=placed,
        out_specs=(P(token + dp, tensor), P(tensor + token + dp, None, None)),
        check_vma=False,
    )
```

```python
import jax
import jax.numpy as jnp
from jax import lax
from jax.experimental import pallas as pl
from jax.experimental.pallas import tpu as pltpu
from jax.sharding import Mesh
from jax.sharding import PartitionSpec as P

HD = 128
THETA_BASE = 500000.0
SIZES = {"xl": 2, "c": 2, "z": 8, "y": 4, "xh": 2}


def shift(x, axis, step=1):
    n = SIZES[axis]
    return lax.ppermute(x, axis, [(i, (i + step) % n) for i in range(n)])


def ring_gather(x, axis):
    n = SIZES[axis]
    out = {0: x}
    ahead, behind = x, x
    for d in range(1, n // 2):
        ahead = shift(ahead, axis, -1)
        behind = shift(behind, axis, 1)
        out[d], out[n - d] = ahead, behind
    half = x.shape[0] // 2
    low = shift(ahead[:half], axis, -1)
    high = shift(behind[half:], axis, 1)
    out[n // 2] = (low, high)
    return out


def xor_order(x, dim, tl, tc):
    shape = x.shape
    x = x.reshape(shape[:dim] + (2, 2) + shape[dim + 1 :])
    x = jnp.where(tl == 1, jnp.flip(x, dim), x)
    x = jnp.where(tc == 1, jnp.flip(x, dim + 1), x)
    return x.reshape(shape)


def place(buffer, block, *at):
    return lax.dynamic_update_slice(buffer, block, at)


def target_kernel(table, w_ref, *refs):
    x_refs, (norm_ref, cos_ref, sin_ref, out_ref) = refs[:4], refs[4:8]
    x_buf, w_buf, acc, sems = refs[8:]
    sources = [x.at[:, h * 1024 : (h + 1) * 1024] for x in x_refs for h in range(2)]
    copies = []
    for i in range(8):
        first = table[i // 2] * 8 + (i % 2) * 4
        x = pltpu.make_async_copy(sources[i], x_buf.at[i], sems.at[0, i])
        w = pltpu.make_async_copy(w_ref.at[pl.ds(first, 4)], w_buf.at[i], sems.at[1, i])
        x.start()
        w.start()
        copies.append((x, w))
    for i, (x, w) in enumerate(copies):
        x.wait()
        w.wait()
        for p in range(2):
            product = jnp.dot(
                x_buf[i],
                w_buf[i, :, p * 256 : (p + 1) * 256].reshape(1024, 256),
                preferred_element_type=jnp.float32,
            )
            acc[p] = product if i == 0 else acc[p] + product
    for p in range(2):
        kv = acc[p] * norm_ref[...]
        for h in range(2):
            head = kv[:, h * HD : (h + 1) * HD]
            if p == 0:
                head = head * cos_ref[...] + pltpu.roll(head, HD // 2, 1) * sin_ref[...]
            cols = slice(p * 256 + h * HD, p * 256 + (h + 1) * HD)
            out_ref[:, cols] = head.astype(jnp.bfloat16)


def targets(table, weight, x, inv_norm, cosine, sine):
    vmem = pl.BlockSpec(memory_space=pltpu.VMEM)
    hbm = pl.BlockSpec(memory_space=pl.ANY)
    return pl.pallas_call(
        target_kernel,
        out_shape=jax.ShapeDtypeStruct((512, 512), jnp.bfloat16),
        in_specs=[pl.BlockSpec(memory_space=pltpu.SMEM)] + [hbm] * 5 + [vmem] * 3,
        out_specs=vmem,
        scratch_shapes=[
            pltpu.VMEM((8, 512, 1024), jnp.bfloat16),
            pltpu.VMEM((8, 4, 512, 256), jnp.bfloat16),
            pltpu.VMEM((2, 512, 256), jnp.float32),
            pltpu.SemaphoreType.DMA((2, 8)),
        ],
        compiler_params=pltpu.CompilerParams(vmem_limit_bytes=56 * 1024 * 1024),
        cost_estimate=pl.CostEstimate(
            flops=2 * 512 * 512 * 8192, bytes_accessed=18 * 1024 * 1024, transcendentals=0
        ),
        name="targets",
    )(table, weight, *x, inv_norm, cosine, sine)


def per_device(hidden_in, sender_cache, block_slot, norm_gain, kv_weight, proj_in, proj_out):
    rows = hidden_in.shape[0]
    tl, tc = lax.axis_index("xl"), lax.axis_index("c")
    z, y, xh = lax.axis_index("z"), lax.axis_index("y"), lax.axis_index("xh")
    tensor = tl * 2 + tc
    bf16, f32 = jnp.bfloat16, jnp.float32
    inv_root = 1.0 / jnp.sqrt(f32(rows * 64))
    zpos = lambda zz: ((zz >> 1) ^ tensor) * 2 + (zz & 1)

    def tensor_gather(own):
        far = shift(own, "xl")
        return [own, shift(own, "c"), far, shift(far, "c")]

    pout = xor_order(proj_out.reshape(8, 2, 4, 256).transpose(2, 0, 1, 3), 0, tl, tc)
    own = jnp.concatenate([proj_in, pout.reshape(32, 512)], axis=0)
    other = shift(own, "xh")
    pair = jnp.stack([jnp.where(xh == 0, own, other), jnp.where(xh == 0, other, own)])
    pair, sender_cache = lax.optimization_barrier((pair, sender_cache))
    pair_in = pair[:, :32].reshape(64, 512)
    pair_out = pair[:, 32:].reshape(2, 4, 8, 512).transpose(1, 0, 2, 3).reshape(64, 512)
    near_in = jnp.zeros((256, 512), bf16)
    near_out = jnp.zeros((4, 64, 512), bf16)
    for d, piece in ring_gather(jnp.concatenate([pair_in, pair_out], axis=0), "y").items():
        yy = (y + d) % 4
        first, second = piece if isinstance(piece, tuple) else (piece[:64], piece[64:])
        near_in = place(near_in, first, yy * 64, 0)
        near_out = place(near_out, second.reshape(4, 16, 512), 0, yy * 16, 0)
    pin_full = jnp.zeros((2048, 512), bf16)
    pout_full = jnp.zeros((4, 512, 512), bf16)
    payload = jnp.concatenate([near_in, near_out.reshape(256, 512)], axis=0)
    for d, piece in ring_gather(payload, "z").items():
        zz = (z + d) % 8
        first, second = piece if isinstance(piece, tuple) else (piece[:256], piece[256:])
        pin_full = place(pin_full, first, zpos(zz) * 256, 0)
        pout_full = place(pout_full, second.reshape(4, 64, 512), 0, zz * 64, 0)

    shard = kv_weight.transpose(1, 0, 2).reshape(512, 256)
    weight = lax.all_gather(shard, ("z", "y"), axis=0, tiled=True).reshape(32, 512, 256)

    cache = jnp.concatenate(tensor_gather(sender_cache), axis=1)
    wide = hidden_in.astype(f32)
    square = jnp.sum(wide * wide, axis=1, keepdims=True)
    square = square + shift(square, "c")
    square = square + shift(square, "xl")
    scaled = (wide * norm_gain[None, :]).astype(bf16)
    scaled, cache = lax.optimization_barrier((scaled, cache))
    features = tensor_gather(scaled)
    inv_norm = lax.rsqrt(square / 8192.0 + 1e-05)
    half = HD // 2
    freqs = THETA_BASE ** (-(jnp.arange(half, dtype=f32) * 2.0 / HD))
    positions = block_slot[0] * rows + jnp.arange(rows, dtype=jnp.int32)
    angles = positions.astype(f32)[:, None] * freqs[None, :]
    cosine, sine = jnp.cos(angles), jnp.sin(angles)
    cosine = jnp.concatenate([cosine, cosine], axis=1)
    sine = jnp.concatenate([-sine, sine], axis=1)
    def half_columns(x, which):
        unit = jnp.arange(256, dtype=jnp.int32)
        source = unit // 32 * 64 + which * 32 + unit % 32
        chosen = jnp.arange(512, dtype=jnp.int32)[:, None] == source[None, :]
        return jnp.dot(x, chosen.astype(bf16), preferred_element_type=f32).astype(bf16)

    pre = jnp.dot(cache, pin_full, preferred_element_type=f32)
    act = jax.nn.silu(pre).astype(bf16)
    partial = [jnp.dot(act, pout_full[r], preferred_element_type=f32) for r in range(4)]
    odd = shift(jnp.concatenate([partial[1], partial[3]], axis=1).astype(bf16), "c")
    mine = partial[0] + odd[:, :512].astype(f32)
    away = (partial[2] + odd[:, 512:].astype(f32)).astype(bf16)
    theirs, features[2] = lax.optimization_barrier((sender_cache, features[2]))
    theirs = shift(half_columns(theirs, 1 - xh), "xh")
    away, theirs, features[3] = lax.optimization_barrier((away, theirs, features[3]))
    pred = mine + shift(away, "xl").astype(f32)
    ours = [half_columns(cache[:, r * 512 : (r + 1) * 512], xh) for r in range(4)]
    ours = jnp.concatenate(ours, axis=1)
    weight, ours = lax.optimization_barrier((weight, ours))
    table = tensor ^ jnp.arange(4, dtype=jnp.int32)
    target = targets(table, weight, features, inv_norm, cosine, sine)
    err = ((pred - target.astype(f32)) * inv_root).astype(bf16)
    errs = tensor_gather(err)
    theirs, *errs = lax.optimization_barrier((theirs, *errs))

    contract_rows = (((0,), (0,)), ((), ()))
    contract_cols = (((1,), (1,)), ((), ()))

    def exchange(g, axis):
        return jnp.sum(lax.all_to_all(g, axis, 0, 0).astype(f32), axis=0)

    def exchange_y(g):
        def part(at):
            return lax.dynamic_slice_in_dim(g, at % 4, 1, axis=1)[:, 0]

        total = part(y).astype(f32)
        for e in (1, 3, 2):
            total = total + shift(part(y + e), "y", e).astype(f32)
        return total

    back = sum(
        lax.dot_general(errs[r], pout_full[r], contract_cols, preferred_element_type=f32)
        for r in range(4)
    )
    sig = jax.nn.sigmoid(pre)
    dpre = (back * sig * (1.0 + pre * (1.0 - sig))).astype(bf16)
    dpre, *errs = lax.optimization_barrier((dpre, *errs))
    their_dpre = shift(dpre, "xh")
    theirs = jnp.concatenate(tensor_gather(theirs), axis=1)
    go = lax.dot_general(
        act, jnp.concatenate(errs, axis=1), contract_rows, preferred_element_type=f32
    )
    go = exchange_y(go.astype(bf16).reshape(8, 4, 16, 2048)).astype(bf16)
    gi = lax.dot_general(ours, dpre, contract_rows, preferred_element_type=f32)
    gi = gi + lax.dot_general(theirs, their_dpre, contract_rows, preferred_element_type=f32)
    gi = gi.astype(bf16).reshape(4, 2, 128, 512)
    gi = xor_order(gi, 0, tl, tc).reshape(8, 128, 512)
    first = exchange(gi[:, :, :256], "z").astype(bf16)
    second = exchange_y(gi[:, :, 256:].reshape(8, 4, 32, 256)).astype(bf16)
    go = go.reshape(8, 2, 8, 2048)
    keep = lax.dynamic_slice_in_dim(go, xh, 1, axis=1)[:, 0]
    give = lax.dynamic_slice_in_dim(go, 1 - xh, 1, axis=1)[:, 0]
    go = (keep.astype(f32) + shift(give, "xh").astype(f32)).astype(bf16)
    first, go = lax.optimization_barrier((first, go))
    first = exchange_y(first.reshape(1, 4, 32, 256))[0]
    last = exchange(jnp.concatenate([second, go.reshape(8, 64, 256)], axis=1), "z")
    grad_in = jnp.concatenate([first, last[:32]], axis=1)
    grad_out = xor_order(last[32:].reshape(8, 4, 2, 256), 1, tl, tc)
    grad_out = grad_out.transpose(0, 2, 1, 3).reshape(8, 2, 1024)
    return grad_in, grad_out


def solution(mesh):
    names = ("xl", "c", "z", "y", "xh")
    fine = Mesh(mesh.devices.reshape(tuple(SIZES[n] for n in names)), names)
    tensor, token, dp = ("xl", "c"), ("z", "y"), ("xh",)
    placed = (
        P(token + dp, tensor),
        P(token + dp, tensor),
        P(token),
        P(tensor),
        P(token, None, tensor),
        P(token + dp, tensor),
        P(tensor + token + dp, None, None),
    )
    return jax.shard_map(
        per_device,
        mesh=fine,
        in_specs=placed,
        out_specs=(P(token + dp, tensor), P(tensor + token + dp, None, None)),
        check_vma=False,
    )
```
